32 devices in a mesh: groups: 2 (over y), tm: 4 (over z), cuts: 2 (over x), col: 2 (over core).
Axes of the slice: x: 2, y: 2, z: 4, core: 2. Of those that a mesh axis runs over, the one named last changes fastest.
Arguments:
- turns: bfloat16 [4096, 4, 1280], P(('groups', 'tm'), 'cuts', 'col'), parts along dimension 0, may hold values from -25 to 25
- shifts: int32 [8], P(('groups', 'tm')), parts along dimension 0, may hold values from -16 to 16
- bands: int32 [8], P(('groups', 'cuts')), parts along dimension 0, may hold values from 2 to 24
- memory: float32 [8], P(('groups', 'cuts')), parts along dimension 0, may hold values from 0.8 to 0.995
Outputs:
- filtered: bfloat16 [8192, 4, 1280], P(('groups', 'tm', 'col'), 'cuts'), parts along dimension 0
The draws below stay inside these ranges and needn't reach their ends.
There are 2 independent parts, one for each index of `groups`. The reference program is written for one: setup_inputs(seed, part) draws one part's arguments, and reference() takes and returns one part's arrays. A program takes and returns all parts, laid end to end along the dimension named above; each array names one. Nothing has to cross between parts.
All inputs are finite; a program needn't handle non-finite values.
Results may differ from the reference program's by a relative error of at most 0.015.
The reference program's roundings to bfloat16 on the way count: a program that leaves them out, or rounds other values in their place, can miss the bound.
Values may be sent and summed in bfloat16 or wider, within the bound.
A program may use at most 64 MiB of HBM per device.

```python
import math
import jax
import jax.numpy as jnp
from jax import lax

ANGLES = 1024
COLUMNS = 1280
BAND_FREQS = 64
HALF = 512
SLICES = 4
WINDOWS = 4


def cycle_pattern(base_key, block_count, amp_low, amp_high):
    col_pos = jnp.arange(COLUMNS, dtype=jnp.int32).astype(jnp.float32)
    low_freq = min(28.0, 0.25 * COLUMNS)
    high_freq = min(52.0, 0.5 * COLUMNS)
    pattern = jnp.zeros((block_count, 1, SLICES, COLUMNS), jnp.float32)
    for term_index in range(6):
        term_keys = jax.random.split(jax.random.fold_in(base_key, term_index), 3)
        wave_freq = jax.random.uniform(term_keys[0], (block_count, 1, SLICES, 1), jnp.float32, low_freq, high_freq)
        wave_amp = jax.random.uniform(term_keys[1], (block_count, 1, SLICES, 1), jnp.float32, amp_low, amp_high)
        wave_phase = jax.random.uniform(term_keys[2], (block_count, 1, SLICES, 1), jnp.float32, -math.pi, math.pi)
        pattern = pattern + wave_amp * jnp.cos(col_pos * (2.0 * math.pi / COLUMNS) * wave_freq + wave_phase)
    return pattern


def draw_turns(key, part):
    subkeys = jax.random.split(jax.random.fold_in(key, 17), 9)
    blocks = WINDOWS
    col_pos = jnp.arange(COLUMNS, dtype=jnp.int32).astype(jnp.float32)
    angle_pos = jnp.arange(blocks * HALF, dtype=jnp.int32).astype(jnp.float32).reshape(blocks, HALF, 1, 1)
    turn_phase = angle_pos * (2.0 * math.pi / ANGLES)
    beam_phase = jax.random.uniform(subkeys[6], (), jnp.float32, -math.pi, math.pi)
    beam_shape = 0.9 + 0.1 * jnp.cos(col_pos * (2.0 * math.pi / COLUMNS) + beam_phase)
    height_low = 1.5
    height_high = 3.0
    base_noise = 0.08 * jax.random.truncated_normal(subkeys[0], -3.0, 3.0, (blocks, HALF, SLICES, COLUMNS), jnp.float32)
    lasting = cycle_pattern(subkeys[2], 1, 0.6, 1.2)
    cycle_part = cycle_pattern(subkeys[1], blocks, 0.6, 1.2) + lasting
    offsets = 0.4 * jax.random.truncated_normal(subkeys[8], -2.5, 2.5, (blocks, HALF, SLICES, 1), jnp.float32)
    object_part = jnp.zeros((blocks, HALF, 1, COLUMNS), jnp.float32)
    for blob_index in range(12):
        blob_keys = jax.random.split(jax.random.fold_in(subkeys[3], blob_index), 4)
        radius = COLUMNS * jax.random.uniform(blob_keys[0], (), jnp.float32, 0.05, 0.4)
        breadth = jnp.maximum(COLUMNS * jax.random.uniform(blob_keys[1], (), jnp.float32, 0.0035, 0.008), 0.8)
        start_phase = jax.random.uniform(blob_keys[2], (), jnp.float32, -math.pi, math.pi)
        height = jax.random.uniform(blob_keys[3], (), jnp.float32, height_low, height_high)
        center = 0.5 * COLUMNS + radius * jnp.cos(turn_phase + start_phase)
        distance = (col_pos - center) / breadth
        object_part = object_part + height * jnp.exp(-0.5 * distance * distance)
    full_field = jnp.clip(base_noise + cycle_part + object_part + offsets * beam_shape, -25.0, 25.0)
    return full_field.reshape(blocks * HALF, SLICES, COLUMNS).astype(jnp.bfloat16)


def place_ends(entries, rng, smallest, high):
    spot = [jax.random.randint(jax.random.fold_in(rng, axis), (), 0, length) for axis, length in enumerate(entries.shape)]
    widest = entries.shape.index(max(entries.shape))
    neighbour = spot[:widest] + [(spot[widest] + 1) % entries.shape[widest]] + spot[widest + 1:]
    return entries.at[tuple(spot)].set(smallest).at[tuple(neighbour)].set(high)


def levels(rng, dims, cuts, least, top_value):
    gain, own = 1.0, jax.random.fold_in(rng, 6)
    for position, blocks in cuts:
        draws = jnp.exp(jax.random.uniform(jax.random.fold_in(own, position), (blocks,), jnp.float32, least / len(cuts), top_value / len(cuts)))
        gain = gain * jnp.repeat(draws, dims[position] // blocks).reshape([-1 if axis == position else 1 for axis in range(len(dims))])
    return gain


def setup_inputs(seed: int = 0, part: int = 0) -> dict:
    arg_keys = jax.random.split(jax.random.key(seed), 5)
    part_keys = jax.random.split(jax.random.fold_in(arg_keys[4], part), 5)
    return {
        "turns": draw_turns(jax.random.fold_in(jax.random.fold_in(arg_keys[4], part), 71), part),
        "shifts": place_ends(jax.random.randint(part_keys[1], (WINDOWS,), -16, 17), jax.random.fold_in(part_keys[1], 1), -16, 16).astype(jnp.int32),
        "bands": place_ends(jax.random.randint(part_keys[2], (SLICES,), 2, 25), jax.random.fold_in(part_keys[2], 1), 2, 24).astype(jnp.int32),
        "memory": jnp.clip(jnp.exp(math.log(0.995) - 0.218131 * jax.random.uniform(part_keys[3], (SLICES,), jnp.float32) ** levels(part_keys[3], (SLICES,), ((0, 2),), -0.2, 0.2)), 0.8, 0.995),
    }


def wave_table(angle_count, freq_count):
    freq_index = lax.broadcasted_iota(jnp.int32, (freq_count, angle_count), 0) + 1
    angle_index = lax.broadcasted_iota(jnp.int32, (freq_count, angle_count), 1)
    phase_int = (freq_index * angle_index) % angle_count
    radians = phase_int.astype(jnp.float32) * (2.0 * math.pi / angle_count)
    return jnp.concatenate([jnp.cos(radians), jnp.sin(radians)], axis=0).astype(jnp.bfloat16)


def damping_weights(bands, freq_count, angle_count):
    freq_values = (jnp.arange(freq_count, dtype=jnp.int32) + 1).astype(jnp.float32)
    band_width = bands.astype(jnp.float32)
    gaussian = jnp.exp(-(freq_values[:, None] ** 2) / (2.0 * band_width[None, :] ** 2)) * (2.0 / angle_count)
    return jnp.concatenate([gaussian, gaussian], axis=0)


def ramp_taps(lag_index, width_total):
    distance = jnp.minimum(lag_index, width_total - lag_index)
    dist_float = jnp.maximum(distance, 1).astype(jnp.float32)
    tap_value = jnp.where(distance == 0, 0.25, jnp.where(distance % 2 == 1, -1.0 / (math.pi ** 2 * dist_float ** 2), 0.0))
    return tap_value.astype(jnp.bfloat16)


def reference(turns, shifts, bands, memory):
    wave_rows = wave_table(ANGLES, BAND_FREQS).astype(jnp.float32)
    weights = damping_weights(bands, BAND_FREQS, ANGLES)
    decay_rate = memory[:, None]
    weighted_sum = jnp.zeros((SLICES, COLUMNS), jnp.float32)
    weight = jnp.zeros((SLICES, 1), jnp.float32)
    previous = jnp.zeros((HALF, SLICES, COLUMNS), jnp.bfloat16)
    column_index = jnp.arange(COLUMNS, dtype=jnp.int32)
    outputs = []
    for window_index in range(WINDOWS):
        current = turns[window_index * HALF:(window_index + 1) * HALF]
        window = jnp.concatenate([previous, current], axis=0)
        flat_window = window.reshape(ANGLES, SLICES * COLUMNS).astype(jnp.float32)
        profile = (jnp.sum(flat_window, axis=0) / ANGLES).reshape(SLICES, COLUMNS)
        weighted_sum = decay_rate * weighted_sum + profile
        weight = decay_rate * weight + 1.0
        estimate = weighted_sum / weight
        padded = jnp.pad(estimate, ((1, 1), (0, 0)))
        cycle = (padded[:-2] + 2.0 * padded[1:-1] + padded[2:]) * 0.25
        spectrum = jnp.dot(wave_rows, flat_window, precision=lax.Precision.HIGHEST)
        scaled = (spectrum.reshape(2 * BAND_FREQS, SLICES, COLUMNS) * weights[:, :, None]).astype(jnp.bfloat16)
        low = jnp.dot(wave_rows.T, scaled.reshape(2 * BAND_FREQS, SLICES * COLUMNS).astype(jnp.float32), precision=lax.Precision.HIGHEST)
        damped = (flat_window - low - cycle.reshape(1, SLICES * COLUMNS)).astype(jnp.bfloat16)
        lag_index = (column_index - shifts[window_index]) % COLUMNS
        taps = ramp_taps(lag_index, COLUMNS).astype(jnp.float32)
        rows_in = damped.astype(jnp.float32).reshape(ANGLES, SLICES, COLUMNS)
        result = jnp.fft.irfft(jnp.fft.rfft(rows_in, axis=2) * jnp.fft.rfft(taps), n=COLUMNS, axis=2)
        outputs.append(result.astype(jnp.bfloat16))
        previous = current
    return jnp.concatenate(outputs, axis=0)
```

```python
import functools
import math

import jax
import jax.numpy as jnp
import ml_dtypes
import numpy as np
from jax import lax
from jax.experimental import pallas as pl
from jax.experimental.pallas import tpu as pltpu
from jax.sharding import PartitionSpec as P

BAND_FREQS = 64
MESH = pl.DeviceIdType.MESH
LANES = 128
F32 = jnp.float32
BF16 = jnp.bfloat16


def tables(half_len, row_count):
    angle_count = 2 * half_len
    freq = np.arange(1, BAND_FREQS + 1, dtype=np.int64)[:, None]
    phase = (freq * np.arange(half_len, dtype=np.int64)[None, :]) % angle_count
    radians = phase.astype(np.float64) * (2.0 * math.pi / angle_count)
    waves = np.concatenate([np.cos(radians), np.sin(radians)], axis=0)
    count = 2 * BAND_FREQS
    wide = np.zeros((row_count, count, half_len, row_count), np.float64)
    ones = np.zeros((16, half_len, row_count), np.float64)
    for s in range(row_count):
        wide[s, :, :, s] = waves
        ones[s, :, s] = 1.0
    wide = wide.reshape(row_count * count, half_len * row_count)
    ones = ones.reshape(16, half_len * row_count)
    cast = lambda v: jnp.asarray(v.astype(np.float32).astype(ml_dtypes.bfloat16))
    return cast(wide), cast(wide.T), cast(ones)


def kernel(sizes, x_ref, wave_ref, wave_t_ref, ones_ref, gain_ref, coef_ref, base_ref, out_ref,
           held, part, other, ramp, acc, sums, est, near, cyc,
           z_send, c_send, recv, p_send, p_recv, s_send, s_recv, e_send, e_recv):
    T, C, R = sizes
    rows, width = x_ref.shape
    chunks = width // LANES
    total = 2 * width
    tm = lax.axis_index("tm")
    cut = lax.axis_index("cuts")
    col = lax.axis_index("col")
    mate = 1 - col

    sums[tm] = jnp.dot(ones_ref[...], x_ref[...], preferred_element_type=F32)[:8]

    barrier = pltpu.get_barrier_semaphore()

    def greet(**where):
        pl.semaphore_signal(barrier, inc=1, device_id=where, device_id_type=MESH)

    for step in range(1, T):
        greet(tm=lax.rem(tm + step, T))
    greet(col=mate)
    for delta in (-1, 1):
        @pl.when((cut + delta >= 0) & (cut + delta < C))
        def _():
            for c in range(2):
                greet(cuts=cut + delta, col=jnp.int32(c))
    cross_up = (col == 1) & (tm < T - 1)
    cross_down = (col == 0) & (tm > 0)

    @pl.when(cross_up)
    def _():
        greet(tm=tm + 1, col=jnp.int32(0))

    @pl.when(cross_down)
    def _():
        greet(tm=tm - 1, col=jnp.int32(1))

    one = lambda flag: jnp.where(flag, 1, 0).astype(jnp.int32)
    pl.semaphore_wait(
        barrier, T + 2 * one(cut > 0) + 2 * one(cut < C - 1) + one(cross_up) + one(cross_down)
    )

    def sum_copy(source, target):
        return pltpu.make_async_remote_copy(
            src_ref=sums.at[source], dst_ref=sums.at[source],
            send_sem=s_send.at[target], recv_sem=s_recv.at[source],
            device_id={"tm": target}, device_id_type=MESH)

    for u in range(T):
        @pl.when(u > tm)
        def _():
            sum_copy(tm, jnp.int32(u)).start()

    def bulk(j, source_col, send_sem, where):
        return pltpu.make_async_remote_copy(
            src_ref=x_ref.at[:, pl.ds(pl.multiple_of(j * LANES, LANES), LANES)],
            dst_ref=held.at[j, :, pl.ds(pl.multiple_of(source_col * LANES, LANES), LANES)],
            send_sem=send_sem.at[j], recv_sem=recv.at[source_col, j],
            device_id=where, device_id_type=MESH)

    def ahead(j):
        return bulk(j, col, z_send, {"tm": lax.rem(tm + 1, T), "col": jnp.int32(0)})

    def across(j):
        return bulk(j, jnp.int32(0), c_send, {"col": mate})

    @pl.when(tm < T - 1)
    def _():
        @pl.loop(0, chunks)
        def _(j):
            ahead(j).start()

    @pl.when(col == 0)
    def _():
        @pl.loop(0, chunks)
        def _(j):
            across(j).start()

    @pl.when(col == 1)
    def _():
        for j in range(chunks):
            held[j, :, LANES:] = x_ref[:, j * LANES:(j + 1) * LANES]

    @pl.when((col == 0) & (tm == 0))
    def _():
        held[...] = jnp.zeros_like(held)

    acc[...] = jnp.zeros_like(acc)

    STEP = 32

    @pl.loop(0, chunks)
    def _(j):
        for c in range(2):
            @pl.loop(0, LANES // STEP)
            def _(k):
                m = lax.broadcasted_iota(jnp.int32, (STEP, total), 0) + (
                    c * width + j * LANES + k * STEP)
                lag = base_ref[...] - m
                lag = jnp.where(lag < 0, lag + total, lag)
                dist = jnp.minimum(lag, total - lag)
                wide = jnp.maximum(dist, 1).astype(F32)
                tap = jnp.where(
                    dist == 0, 0.25,
                    jnp.where((dist & 1) == 1, -1.0 / (math.pi**2 * wide * wide), 0.0))
                ramp[j, pl.ds(pl.multiple_of(c * LANES + k * STEP, STEP), STEP), :] = tap.astype(BF16)

    est[...] = jnp.zeros_like(est)
    for u in range(T):
        @pl.when(u < tm)
        def _():
            sum_copy(jnp.int32(u), lax.rem(tm + 1, T)).wait_recv()

        @pl.when(u <= tm)
        def _():
            est[...] += coef_ref[u] * sums[u]
    near[1, col] = est[...]

    def est_copy(delta, to_col, from_col):
        return pltpu.make_async_remote_copy(
            src_ref=est, dst_ref=near.at[1 - delta, from_col],
            send_sem=e_send.at[1 - delta, to_col], recv_sem=e_recv.at[1 - delta, from_col],
            device_id={"cuts": cut + delta, "col": to_col}, device_id_type=MESH)

    est_copy(0, mate, col).start()
    for delta in (-1, 1):
        @pl.when((cut + delta >= 0) & (cut + delta < C))
        def _():
            for c in range(2):
                est_copy(delta, jnp.int32(c), col).start()

    def part_copy(j):
        return pltpu.make_async_remote_copy(
            src_ref=part.at[j], dst_ref=other.at[j],
            send_sem=p_send.at[j], recv_sem=p_recv.at[j],
            device_id={"col": mate}, device_id_type=MESH)

    def gather(j):
        @pl.when((col == 1) | (tm > 0))
        def _():
            bulk(j, jnp.int32(0), z_send, {"col": mate}).wait_recv()

        @pl.when((col == 0) & (tm > 0))
        def _():
            bulk(j, jnp.int32(1), z_send, {"col": mate}).wait_recv()

        part[j] = jnp.dot(wave_ref[...], held[j], preferred_element_type=F32)
        part_copy(j).start()

    gather(0)

    est_copy(0, mate, mate).wait_recv()
    for delta in (-1, 1):
        @pl.when((cut - delta >= 0) & (cut - delta < C))
        def _():
            for c in range(2):
                pltpu.make_async_remote_copy(
                    src_ref=est, dst_ref=near.at[1 - delta, c],
                    send_sem=e_send.at[1 - delta, c], recv_sem=e_recv.at[1 - delta, c],
                    device_id={"cuts": cut - delta, "col": jnp.int32(c)},
                    device_id_type=MESH).wait_recv()

        @pl.when((cut - delta < 0) | (cut - delta >= C))
        def _():
            near[1 - delta] = jnp.zeros_like(near[1 - delta])

    for c in range(2):
        edge = [near[0, c, R - 1:R, :]] + [near[1, c, s:s + 1, :] for s in range(R)] + [near[2, c, 0:1, :]]
        for s in range(R):
            line = (edge[s] + 2.0 * edge[s + 1] + edge[s + 2]) * 0.25
            for j in range(chunks):
                cyc[j, s:s + 1, c * LANES:(c + 1) * LANES] = line[:, j * LANES:(j + 1) * LANES]

    TILE = 256

    def filt(j, last):
        part_copy(j).wait_recv()
        scaled = (gain_ref[0] * part[j] + gain_ref[1] * other[j]).astype(BF16)
        which = lax.broadcasted_iota(jnp.int32, (TILE, 2 * LANES), 0) % R
        shade = jnp.zeros((TILE, 2 * LANES), F32)
        for s in range(R):
            shade = jnp.where(which == s, cyc[j, s:s + 1, :], shade)

        @pl.loop(0, rows // TILE)
        def _(k):
            tile = pl.ds(pl.multiple_of(k * TILE, TILE), TILE)
            low = jnp.dot(wave_t_ref[tile, :], scaled, preferred_element_type=F32)
            damped = (held[j, tile, :].astype(F32) - low - shade).astype(BF16)
            product = acc[tile, :] + jnp.dot(damped, ramp[j], preferred_element_type=F32)
            if last:
                out_ref[tile, :] = product.astype(BF16)
            else:
                acc[tile, :] = product

    @pl.loop(1, chunks)
    def _(j):
        gather(j)
        filt(j - 1, False)

    filt(chunks - 1, True)

    for u in range(T):
        @pl.when(u > tm)
        def _():
            sum_copy(tm, jnp.int32(u)).wait_send()
    est_copy(0, mate, col).wait_send()
    for delta in (-1, 1):
        @pl.when((cut + delta >= 0) & (cut + delta < C))
        def _():
            for c in range(2):
                est_copy(delta, jnp.int32(c), col).wait_send()

    @pl.loop(0, chunks)
    def _(j):
        part_copy(j).wait_send()

        @pl.when(tm < T - 1)
        def _():
            ahead(j).wait_send()

        @pl.when(col == 0)
        def _():
            across(j).wait_send()


def local(turns, shifts, bands, memory):
    half_len, R, width = turns.shape
    T, C = lax.axis_size("tm"), lax.axis_size("cuts")
    tm = lax.axis_index("tm")
    rows, total, chunks = half_len * R, 2 * width, width // LANES
    angle_count = 2 * half_len
    count = 2 * BAND_FREQS
    wide, wide_t, ones = tables(half_len, R)
    flat = turns.reshape(rows, width)

    freq = np.arange(1, BAND_FREQS + 1, dtype=np.float32)
    freq = np.concatenate([freq, freq])
    sign = np.where(freq % 2 == 1, -1.0, 1.0).astype(np.float32)
    gain = jnp.exp(-(freq[None, :] ** 2) / (2.0 * bands.astype(F32)[:, None] ** 2)) * (2.0 / angle_count)
    gains = jnp.stack([gain.reshape(R * count, 1), (gain * sign[None, :]).reshape(R * count, 1)])

    lag = tm - jnp.arange(T + 1, dtype=jnp.int32)
    powers = jnp.where(
        lag[:, None] >= 0,
        jnp.power(memory[None, :], jnp.maximum(lag, 0).astype(F32)[:, None]), 0.0)
    coef = (powers[:-1] + powers[1:]) / (jnp.sum(powers, axis=0)[None, :] * angle_count)
    coef = jnp.pad(coef, ((0, 0), (0, 8 - R)))[:, :, None]
    base = ((jnp.arange(total, dtype=jnp.int32) - shifts[0]) % total)[None, :]

    vmem = pl.BlockSpec(memory_space=pltpu.VMEM)
    dma = pltpu.SemaphoreType.DMA
    out = pl.pallas_call(
        functools.partial(kernel, (T, C, R)),
        out_shape=jax.ShapeDtypeStruct((rows, total), BF16),
        in_specs=[vmem] * 7,
        out_specs=vmem,
        scratch_shapes=[
            pltpu.VMEM((chunks, rows, 2 * LANES), BF16),
            pltpu.VMEM((chunks, R * count, 2 * LANES), F32),
            pltpu.VMEM((chunks, R * count, 2 * LANES), F32),
            pltpu.VMEM((chunks, 2 * LANES, total), BF16),
            pltpu.VMEM((rows, total), F32),
            pltpu.VMEM((T, 8, width), F32),
            pltpu.VMEM((8, width), F32),
            pltpu.VMEM((3, 2, 8, width), F32),
            pltpu.VMEM((chunks, 8, 2 * LANES), F32),
            dma((chunks,)), dma((chunks,)), dma((2, chunks)),
            dma((chunks,)), dma((chunks,)),
            dma((T,)), dma((T,)), dma((3, 2)), dma((3, 2)),
        ],
        compiler_params=pltpu.CompilerParams(
            collective_id=0, has_side_effects=True, vmem_limit_bytes=48 * 1024 * 1024),
        cost_estimate=pl.CostEstimate(
            flops=2 * rows * total * (total + 2 * R * count),
            bytes_accessed=8 * rows * total, transcendentals=0),
    )(flat, wide, wide_t, ones, gains, coef, base)
    return out.reshape(half_len, R, total)


def solution(mesh):
    placed = (
        P(("groups", "tm"), "cuts", "col"),
        P(("groups", "tm")),
        P(("groups", "cuts")),
        P(("groups", "cuts")),
    )
    return jax.shard_map(
        local,
        mesh=mesh,
        in_specs=placed,
        out_specs=P(("groups", "tm", "col"), "cuts", None),
        check_vma=False,
    )
```

```python
import functools
import math

import jax
import jax.numpy as jnp
import ml_dtypes
import numpy as np
from jax import lax
from jax.experimental import pallas as pl
from jax.experimental.pallas import tpu as pltpu
from jax.sharding import PartitionSpec as P

BAND_FREQS = 64
MESH = pl.DeviceIdType.MESH
LANES = 128
DEPTH = 2
F32 = jnp.float32
BF16 = jnp.bfloat16


def tables(half_len, row_count):
    angle_count = 2 * half_len
    freq = np.arange(1, BAND_FREQS + 1, dtype=np.int64)[:, None]
    phase = (freq * np.arange(half_len, dtype=np.int64)[None, :]) % angle_count
    radians = phase.astype(np.float64) * (2.0 * math.pi / angle_count)
    waves = np.concatenate([np.cos(radians), np.sin(radians)], axis=0)
    count = 2 * BAND_FREQS
    wide = np.zeros((row_count, count, half_len, row_count), np.float64)
    ones = np.zeros((16, half_len, row_count), np.float64)
    for s in range(row_count):
        wide[s, :, :, s] = waves
        ones[s, :, s] = 1.0
    wide = wide.reshape(row_count * count, half_len * row_count)
    ones = ones.reshape(16, half_len * row_count)
    cast = lambda v: jnp.asarray(v.astype(np.float32).astype(ml_dtypes.bfloat16))
    return cast(wide), cast(wide.T), cast(ones)


def kernel(sizes, x_ref, wave_ref, wave_t_ref, ones_ref, shift_ref, band_ref, memory_ref, out_ref,
           held, part, other, ramp, acc, sums, est, near, cyc, gain_ref, weight,
           z_send, c_send, recv, p_send, p_recv, s_send, s_recv, e_send, e_recv):
    T, C, R = sizes
    rows, width = x_ref.shape
    chunks = width // LANES
    total = 2 * width
    tm = lax.axis_index("tm")
    cut = lax.axis_index("cuts")
    col = lax.axis_index("col")
    mate = 1 - col

    sums[tm] = jnp.dot(ones_ref[...], x_ref[...], preferred_element_type=F32)[:8]

    barrier = pltpu.get_barrier_semaphore()

    def greet(**where):
        pl.semaphore_signal(barrier, inc=1, device_id=where, device_id_type=MESH)

    for step in range(1, T):
        greet(tm=lax.rem(tm + step, T))
    greet(col=mate)
    for delta in (-1, 1):
        @pl.when((cut + delta >= 0) & (cut + delta < C))
        def _():
            for c in range(2):
                greet(cuts=cut + delta, col=jnp.int32(c))
    cross_up = (col == 1) & (tm < T - 1)
    cross_down = (col == 0) & (tm > 0)

    @pl.when(cross_up)
    def _():
        greet(tm=tm + 1, col=jnp.int32(0))

    @pl.when(cross_down)
    def _():
        greet(tm=tm - 1, col=jnp.int32(1))

    one = lambda flag: jnp.where(flag, 1, 0).astype(jnp.int32)
    pl.semaphore_wait(
        barrier, T + 2 * one(cut > 0) + 2 * one(cut < C - 1) + one(cross_up) + one(cross_down)
    )

    def sum_copy(source, target):
        return pltpu.make_async_remote_copy(
            src_ref=sums.at[source], dst_ref=sums.at[source],
            send_sem=s_send.at[target], recv_sem=s_recv.at[source],
            device_id={"tm": target}, device_id_type=MESH)

    for u in range(T):
        @pl.when(u > tm)
        def _():
            sum_copy(tm, jnp.int32(u)).start()

    def bulk(j, source_col, send_sem, where):
        return pltpu.make_async_remote_copy(
            src_ref=x_ref.at[:, pl.ds(pl.multiple_of(j * LANES, LANES), LANES)],
            dst_ref=held.at[j, :, pl.ds(pl.multiple_of(source_col * LANES, LANES), LANES)],
            send_sem=send_sem.at[j], recv_sem=recv.at[source_col, j],
            device_id=where, device_id_type=MESH)

    def ahead(j):
        return bulk(j, col, z_send, {"tm": lax.rem(tm + 1, T), "col": jnp.int32(0)})

    def across(j):
        return bulk(j, jnp.int32(0), c_send, {"col": mate})

    @pl.when(tm < T - 1)
    def _():
        for j in range(min(DEPTH, chunks)):
            ahead(jnp.int32(j)).start()

    @pl.when(col == 0)
    def _():
        @pl.loop(0, chunks)
        def _(j):
            across(j).start()

    @pl.when(col == 1)
    def _():
        for j in range(chunks):
            held[j, :, LANES:] = x_ref[:, j * LANES:(j + 1) * LANES]

    @pl.when((col == 0) & (tm == 0))
    def _():
        held[...] = jnp.zeros_like(held)

    acc[...] = jnp.zeros_like(acc)

    count = 2 * BAND_FREQS
    index = lax.broadcasted_iota(jnp.int32, (R * count, 1), 0)
    band = jnp.zeros((R * count, 1), F32)
    for s in range(R):
        band = jnp.where(index // count == s, band_ref[s].astype(F32), band)
    freq = index % BAND_FREQS + 1
    wave = freq.astype(F32)
    gain = jnp.exp(-(wave * wave) / (2.0 * band * band)) * (2.0 / (2 * (rows // R)))
    gain_ref[0] = gain
    gain_ref[1] = jnp.where(freq % 2 == 1, -gain, gain)

    STEP = 32

    target = lax.broadcasted_iota(jnp.int32, (1, total), 1) - shift_ref[0]
    target = jnp.where(target < 0, target + total, target)
    target = jnp.where(target >= total, target - total, target)

    @pl.loop(0, chunks)
    def _(j):
        for c in range(2):
            @pl.loop(0, LANES // STEP)
            def _(k):
                m = lax.broadcasted_iota(jnp.int32, (STEP, total), 0) + (
                    c * width + j * LANES + k * STEP)
                lag = target - m
                lag = jnp.where(lag < 0, lag + total, lag)
                dist = jnp.minimum(lag, total - lag)
                wide = jnp.maximum(dist, 1).astype(F32)
                tap = jnp.where(
                    dist == 0, 0.25,
                    jnp.where((dist & 1) == 1, -1.0 / (math.pi**2 * wide * wide), 0.0))
                ramp[j, pl.ds(pl.multiple_of(c * LANES + k * STEP, STEP), STEP), :] = tap.astype(BF16)

    line_index = lax.broadcasted_iota(jnp.int32, (8, 1), 0)
    decay = jnp.zeros((8, 1), F32)
    for s in range(R):
        decay = jnp.where(line_index == s, memory_ref[s], decay)
    est[...] = jnp.zeros_like(est)
    weight[...] = jnp.zeros_like(weight)
    for u in range(T):
        @pl.when(u < tm)
        def _():
            sum_copy(jnp.int32(u), lax.rem(tm + 1, T)).wait_recv()

        @pl.when(u <= tm)
        def _():
            both = sums[u] if u == 0 else sums[u - 1] + sums[u]
            est[...] = decay * est[...] + both * (1.0 / (2 * (rows // R)))
            weight[...] = decay * weight[...] + 1.0
    est[...] = est[...] / weight[...]
    near[1, col] = est[...]

    def est_copy(delta, to_col, from_col):
        return pltpu.make_async_remote_copy(
            src_ref=est, dst_ref=near.at[1 - delta, from_col],
            send_sem=e_send.at[1 - delta, to_col], recv_sem=e_recv.at[1 - delta, from_col],
            device_id={"cuts": cut + delta, "col": to_col}, device_id_type=MESH)

    est_copy(0, mate, col).start()
    for delta in (-1, 1):
        @pl.when((cut + delta >= 0) & (cut + delta < C))
        def _():
            for c in range(2):
                est_copy(delta, jnp.int32(c), col).start()

    def part_copy(j):
        return pltpu.make_async_remote_copy(
            src_ref=part.at[j], dst_ref=other.at[j],
            send_sem=p_send.at[j], recv_sem=p_recv.at[j],
            device_id={"col": mate}, device_id_type=MESH)

    def gather(j):
        @pl.when((col == 1) | (tm > 0))
        def _():
            bulk(j, jnp.int32(0), z_send, {"col": mate}).wait_recv()

        @pl.when((col == 0) & (tm > 0))
        def _():
            bulk(j, jnp.int32(1), z_send, {"col": mate}).wait_recv()

        @pl.when(tm < T - 1)
        def _():
            ahead(j).wait_send()

            @pl.when(j + DEPTH < chunks)
            def _():
                ahead(j + DEPTH).start()

        part[j] = jnp.dot(wave_ref[...], held[j], preferred_element_type=F32)
        part_copy(j).start()

    gather(jnp.int32(0))

    est_copy(0, mate, mate).wait_recv()
    for delta in (-1, 1):
        @pl.when((cut - delta >= 0) & (cut - delta < C))
        def _():
            for c in range(2):
                pltpu.make_async_remote_copy(
                    src_ref=est, dst_ref=near.at[1 - delta, c],
                    send_sem=e_send.at[1 - delta, c], recv_sem=e_recv.at[1 - delta, c],
                    device_id={"cuts": cut - delta, "col": jnp.int32(c)},
                    device_id_type=MESH).wait_recv()

        @pl.when((cut - delta < 0) | (cut - delta >= C))
        def _():
            near[1 - delta] = jnp.zeros_like(near[1 - delta])

    for c in range(2):
        edge = [near[0, c, R - 1:R, :]] + [near[1, c, s:s + 1, :] for s in range(R)] + [near[2, c, 0:1, :]]
        for s in range(R):
            line = (edge[s] + 2.0 * edge[s + 1] + edge[s + 2]) * 0.25
            for j in range(chunks):
                cyc[j, s:s + 1, c * LANES:(c + 1) * LANES] = line[:, j * LANES:(j + 1) * LANES]

    TILE = 256

    def filt(j, last):
        part_copy(j).wait_recv()
        scaled = (gain_ref[0] * part[j] + gain_ref[1] * other[j]).astype(BF16)
        which = lax.broadcasted_iota(jnp.int32, (TILE, 2 * LANES), 0) % R
        shade = jnp.zeros((TILE, 2 * LANES), F32)
        for s in range(R):
            shade = jnp.where(which == s, cyc[j, s:s + 1, :], shade)

        @pl.loop(0, rows // TILE)
        def _(k):
            tile = pl.ds(pl.multiple_of(k * TILE, TILE), TILE)
            low = jnp.dot(wave_t_ref[tile, :], scaled, preferred_element_type=F32)
            damped = (held[j, tile, :].astype(F32) - low - shade).astype(BF16)
            product = acc[tile, :] + jnp.dot(damped, ramp[j], preferred_element_type=F32)
            if last:
                out_ref[tile, :] = product.astype(BF16)
            else:
                acc[tile, :] = product

    @pl.loop(1, chunks)
    def _(j):
        gather(j)
        filt(j - 1, False)

    filt(chunks - 1, True)

    for u in range(T):
        @pl.when(u > tm)
        def _():
            sum_copy(tm, jnp.int32(u)).wait_send()
    est_copy(0, mate, col).wait_send()
    for delta in (-1, 1):
        @pl.when((cut + delta >= 0) & (cut + delta < C))
        def _():
            for c in range(2):
                est_copy(delta, jnp.int32(c), col).wait_send()

    @pl.loop(0, chunks)
    def _(j):
        part_copy(j).wait_send()

        @pl.when(col == 0)
        def _():
            across(j).wait_send()


def local(turns, shifts, bands, memory):
    half_len, R, width = turns.shape
    T, C = lax.axis_size("tm"), lax.axis_size("cuts")
    rows, total, chunks = half_len * R, 2 * width, width // LANES
    count = 2 * BAND_FREQS
    wide, wide_t, ones = tables(half_len, R)
    flat = turns.reshape(rows, width)

    vmem = pl.BlockSpec(memory_space=pltpu.VMEM)
    dma = pltpu.SemaphoreType.DMA
    out = pl.pallas_call(
        functools.partial(kernel, (T, C, R)),
        out_shape=jax.ShapeDtypeStruct((rows, total), BF16),
        in_specs=[vmem] * 4 + [pl.BlockSpec(memory_space=pltpu.SMEM)] * 3,
        out_specs=vmem,
        scratch_shapes=[
            pltpu.VMEM((chunks, rows, 2 * LANES), BF16),
            pltpu.VMEM((chunks, R * count, 2 * LANES), F32),
            pltpu.VMEM((chunks, R * count, 2 * LANES), F32),
            pltpu.VMEM((chunks, 2 * LANES, total), BF16),
            pltpu.VMEM((rows, total), F32),
            pltpu.VMEM((T, 8, width), F32),
            pltpu.VMEM((8, width), F32),
            pltpu.VMEM((3, 2, 8, width), F32),
            pltpu.VMEM((chunks, 8, 2 * LANES), F32),
            pltpu.VMEM((2, R * count, 1), F32),
            pltpu.VMEM((8, 1), F32),
            dma((chunks,)), dma((chunks,)), dma((2, chunks)),
            dma((chunks,)), dma((chunks,)),
            dma((T,)), dma((T,)), dma((3, 2)), dma((3, 2)),
        ],
        compiler_params=pltpu.CompilerParams(
            collective_id=0, has_side_effects=True, vmem_limit_bytes=48 * 1024 * 1024),
        cost_estimate=pl.CostEstimate(
            flops=2 * rows * total * (total + 2 * R * count),
            bytes_accessed=8 * rows * total, transcendentals=0),
    )(flat, wide, wide_t, ones, shifts, bands, memory)
    return out.reshape(half_len, R, total)


def solution(mesh):
    placed = (
        P(("groups", "tm"), "cuts", "col"),
        P(("groups", "tm")),
        P(("groups", "cuts")),
        P(("groups", "cuts")),
    )
    return jax.shard_map(
        local,
        mesh=mesh,
        in_specs=placed,
        out_specs=P(("groups", "tm", "col"), "cuts", None),
        check_vma=False,
    )
```

```python
import functools
import math

import jax
import jax.numpy as jnp
import ml_dtypes
import numpy as np
from jax import lax
from jax.experimental import pallas as pl
from jax.experimental.pallas import tpu as pltpu
from jax.sharding import PartitionSpec as P

BAND_FREQS = 64
MESH = pl.DeviceIdType.MESH
LANES = 128
DEPTH = 2
F32 = jnp.float32
BF16 = jnp.bfloat16


def tables(half_len, row_count):
    angle_count = 2 * half_len
    freq = np.arange(1, BAND_FREQS + 1, dtype=np.int64)[:, None]
    phase = (freq * np.arange(half_len, dtype=np.int64)[None, :]) % angle_count
    radians = phase.astype(np.float64) * (2.0 * math.pi / angle_count)
    waves = np.concatenate([np.cos(radians), np.sin(radians)], axis=0)
    count = 2 * BAND_FREQS
    wide = np.zeros((row_count, count, half_len, row_count), np.float64)
    ones = np.zeros((16, half_len, row_count), np.float64)
    for s in range(row_count):
        wide[s, :, :, s] = waves
        ones[s, :, s] = 1.0
    wide = wide.reshape(row_count * count, half_len * row_count)
    ones = ones.reshape(16, half_len * row_count)
    cast = lambda v: jnp.asarray(v.astype(np.float32).astype(ml_dtypes.bfloat16))
    return cast(wide), cast(wide.T), cast(ones)


def kernel(sizes, x_ref, wave_ref, wave_t_ref, ones_ref, shift_ref, band_ref, memory_ref, out_ref,
           held, own, part, other, ramp, acc, sums, est, near, cyc, gain_ref, weight,
           l_sem, z_send, c_send, recv, p_send, p_recv, s_send, s_recv, e_send, e_recv):
    T, C, R = sizes
    half_len, chunks, _, _ = x_ref.shape
    rows, width = half_len * R, chunks * LANES
    total = 2 * width
    tm = lax.axis_index("tm")
    cut = lax.axis_index("cuts")
    col = lax.axis_index("col")
    mate = 1 - col

    def mine(j):
        return pltpu.make_async_copy(x_ref.at[:, j], own.at[j], l_sem.at[0, j])

    def kept(j):
        return pltpu.make_async_copy(x_ref.at[:, j], held.at[j, 1], l_sem.at[1, j])

    def flat(ref):
        return ref.reshape(rows, LANES)

    for j in range(chunks):
        mine(j).start()

    barrier = pltpu.get_barrier_semaphore()

    def greet(**where):
        pl.semaphore_signal(barrier, inc=1, device_id=where, device_id_type=MESH)

    for step in range(1, T):
        greet(tm=lax.rem(tm + step, T))
    greet(col=mate)
    for delta in (-1, 1):
        @pl.when((cut + delta >= 0) & (cut + delta < C))
        def _():
            for c in range(2):
                greet(cuts=cut + delta, col=jnp.int32(c))
    cross_up = (col == 1) & (tm < T - 1)
    cross_down = (col == 0) & (tm > 0)

    @pl.when(cross_up)
    def _():
        greet(tm=tm + 1, col=jnp.int32(0))

    @pl.when(cross_down)
    def _():
        greet(tm=tm - 1, col=jnp.int32(1))

    one = lambda flag: jnp.where(flag, 1, 0).astype(jnp.int32)
    pl.semaphore_wait(
        barrier, T + 2 * one(cut > 0) + 2 * one(cut < C - 1) + one(cross_up) + one(cross_down)
    )

    def sum_copy(source, target):
        return pltpu.make_async_remote_copy(
            src_ref=sums.at[source], dst_ref=sums.at[source],
            send_sem=s_send.at[target], recv_sem=s_recv.at[source],
            device_id={"tm": target}, device_id_type=MESH)

    def bulk(j, source_col, send_sem, where):
        return pltpu.make_async_remote_copy(
            src_ref=x_ref.at[:, j],
            dst_ref=held.at[j, source_col],
            send_sem=send_sem.at[j], recv_sem=recv.at[source_col, j],
            device_id=where, device_id_type=MESH)

    def ahead(j):
        return bulk(j, col, z_send, {"tm": lax.rem(tm + 1, T), "col": jnp.int32(0)})

    def across(j):
        return bulk(j, jnp.int32(0), c_send, {"col": mate})

    @pl.when(tm < T - 1)
    def _():
        for j in range(min(DEPTH, chunks)):
            ahead(jnp.int32(j)).start()

    @pl.when(col == 0)
    def _():
        @pl.loop(0, chunks)
        def _(j):
            across(j).start()

    @pl.when(col == 1)
    def _():
        for j in range(chunks):
            kept(j).start()

    for j in range(chunks):
        mine(j).wait()
        sums[tm, :, j * LANES:(j + 1) * LANES] = jnp.dot(
            ones_ref[...], flat(own.at[j])[...], preferred_element_type=F32)[:8]

    for u in range(T):
        @pl.when(u > tm)
        def _():
            sum_copy(tm, jnp.int32(u)).start()

    @pl.when((col == 0) & (tm == 0))
    def _():
        held[...] = jnp.zeros_like(held)

    acc[...] = jnp.zeros_like(acc)

    count = 2 * BAND_FREQS
    index = lax.broadcasted_iota(jnp.int32, (R * count, 1), 0)
    band = jnp.zeros((R * count, 1), F32)
    for s in range(R):
        band = jnp.where(index // count == s, band_ref[s].astype(F32), band)
    freq = index % BAND_FREQS + 1
    wave = freq.astype(F32)
    gain = jnp.exp(-(wave * wave) / (2.0 * band * band)) * (2.0 / (2 * (rows // R)))
    gain_ref[0] = gain
    gain_ref[1] = jnp.where(freq % 2 == 1, -gain, gain)

    STEP = 32

    target = lax.broadcasted_iota(jnp.int32, (1, total), 1) - shift_ref[0]
    target = jnp.where(target < 0, target + total, target)
    target = jnp.where(target >= total, target - total, target)

    @pl.loop(0, chunks)
    def _(j):
        for c in range(2):
            @pl.loop(0, LANES // STEP)
            def _(k):
                m = lax.broadcasted_iota(jnp.int32, (STEP, total), 0) + (
                    c * width + j * LANES + k * STEP)
                lag = target - m
                lag = jnp.where(lag < 0, lag + total, lag)
                dist = jnp.minimum(lag, total - lag)
                wide = jnp.maximum(dist, 1).astype(F32)
                tap = jnp.where(
                    dist == 0, 0.25,
                    jnp.where((dist & 1) == 1, -1.0 / (math.pi**2 * wide * wide), 0.0))
                ramp[j, pl.ds(pl.multiple_of(c * LANES + k * STEP, STEP), STEP), :] = tap.astype(BF16)

    line_index = lax.broadcasted_iota(jnp.int32, (8, 1), 0)
    decay = jnp.zeros((8, 1), F32)
    for s in range(R):
        decay = jnp.where(line_index == s, memory_ref[s], decay)
    est[...] = jnp.zeros_like(est)
    weight[...] = jnp.zeros_like(weight)
    for u in range(T):
        @pl.when(u < tm)
        def _():
            sum_copy(jnp.int32(u), lax.rem(tm + 1, T)).wait_recv()

        @pl.when(u <= tm)
        def _():
            both = sums[u] if u == 0 else sums[u - 1] + sums[u]
            est[...] = decay * est[...] + both * (1.0 / (2 * (rows // R)))
            weight[...] = decay * weight[...] + 1.0
    est[...] = est[...] / weight[...]
    near[1, col] = est[...]

    def est_copy(delta, to_col, from_col):
        return pltpu.make_async_remote_copy(
            src_ref=est, dst_ref=near.at[1 - delta, from_col],
            send_sem=e_send.at[1 - delta, to_col], recv_sem=e_recv.at[1 - delta, from_col],
            device_id={"cuts": cut + delta, "col": to_col}, device_id_type=MESH)

    est_copy(0, mate, col).start()
    for delta in (-1, 1):
        @pl.when((cut + delta >= 0) & (cut + delta < C))
        def _():
            for c in range(2):
                est_copy(delta, jnp.int32(c), col).start()

    def part_copy(j):
        return pltpu.make_async_remote_copy(
            src_ref=part.at[j], dst_ref=other.at[j],
            send_sem=p_send.at[j], recv_sem=p_recv.at[j],
            device_id={"col": mate}, device_id_type=MESH)

    def gather(j):
        @pl.when((col == 1) | (tm > 0))
        def _():
            bulk(j, jnp.int32(0), z_send, {"col": mate}).wait_recv()

        @pl.when((col == 0) & (tm > 0))
        def _():
            bulk(j, jnp.int32(1), z_send, {"col": mate}).wait_recv()

        @pl.when(tm < T - 1)
        def _():
            ahead(j).wait_send()

            @pl.when(j + DEPTH < chunks)
            def _():
                ahead(j + DEPTH).start()

        @pl.when(col == 1)
        def _():
            kept(j).wait()

        both = jnp.concatenate([flat(held.at[j, c])[...] for c in range(2)], axis=1)
        part[j] = jnp.dot(wave_ref[...], both, preferred_element_type=F32)
        part_copy(j).start()

    gather(jnp.int32(0))

    est_copy(0, mate, mate).wait_recv()
    for delta in (-1, 1):
        @pl.when((cut - delta >= 0) & (cut - delta < C))
        def _():
            for c in range(2):
                pltpu.make_async_remote_copy(
                    src_ref=est, dst_ref=near.at[1 - delta, c],
                    send_sem=e_send.at[1 - delta, c], recv_sem=e_recv.at[1 - delta, c],
                    device_id={"cuts": cut - delta, "col": jnp.int32(c)},
                    device_id_type=MESH).wait_recv()

        @pl.when((cut - delta < 0) | (cut - delta >= C))
        def _():
            near[1 - delta] = jnp.zeros_like(near[1 - delta])

    for c in range(2):
        edge = [near[0, c, R - 1:R, :]] + [near[1, c, s:s + 1, :] for s in range(R)] + [near[2, c, 0:1, :]]
        for s in range(R):
            line = (edge[s] + 2.0 * edge[s + 1] + edge[s + 2]) * 0.25
            for j in range(chunks):
                cyc[j, s:s + 1, c * LANES:(c + 1) * LANES] = line[:, j * LANES:(j + 1) * LANES]

    TILE = 256

    def filt(j, last):
        part_copy(j).wait_recv()
        scaled = (gain_ref[0] * part[j] + gain_ref[1] * other[j]).astype(BF16)
        which = lax.broadcasted_iota(jnp.int32, (TILE, 2 * LANES), 0) % R
        shade = jnp.zeros((TILE, 2 * LANES), F32)
        for s in range(R):
            shade = jnp.where(which == s, cyc[j, s:s + 1, :], shade)

        @pl.loop(0, rows // TILE)
        def _(k):
            tile = pl.ds(pl.multiple_of(k * TILE, TILE), TILE)
            low = jnp.dot(wave_t_ref[tile, :], scaled, preferred_element_type=F32)
            both = jnp.concatenate([flat(held.at[j, c])[tile, :] for c in range(2)], axis=1)
            damped = (both.astype(F32) - low - shade).astype(BF16)
            product = acc[tile, :] + jnp.dot(damped, ramp[j], preferred_element_type=F32)
            if last:
                out_ref[tile, :] = product.astype(BF16)
            else:
                acc[tile, :] = product

    @pl.loop(1, chunks)
    def _(j):
        gather(j)
        filt(j - 1, False)

    filt(chunks - 1, True)

    for u in range(T):
        @pl.when(u > tm)
        def _():
            sum_copy(tm, jnp.int32(u)).wait_send()
    est_copy(0, mate, col).wait_send()
    for delta in (-1, 1):
        @pl.when((cut + delta >= 0) & (cut + delta < C))
        def _():
            for c in range(2):
                est_copy(delta, jnp.int32(c), col).wait_send()

    @pl.loop(0, chunks)
    def _(j):
        part_copy(j).wait_send()

        @pl.when(col == 0)
        def _():
            across(j).wait_send()


def local(turns, shifts, bands, memory):
    half_len, R, width = turns.shape
    T, C = lax.axis_size("tm"), lax.axis_size("cuts")
    rows, total, chunks = half_len * R, 2 * width, width // LANES
    count = 2 * BAND_FREQS
    wide, wide_t, ones = tables(half_len, R)
    pieces = turns.reshape(half_len, R, chunks, LANES).transpose(0, 2, 1, 3)

    vmem = pl.BlockSpec(memory_space=pltpu.VMEM)
    dma = pltpu.SemaphoreType.DMA
    out = pl.pallas_call(
        functools.partial(kernel, (T, C, R)),
        out_shape=jax.ShapeDtypeStruct((rows, total), BF16),
        in_specs=[pl.BlockSpec(memory_space=pl.ANY)] + [vmem] * 3 + [pl.BlockSpec(memory_space=pltpu.SMEM)] * 3,
        out_specs=vmem,
        scratch_shapes=[
            pltpu.VMEM((chunks, 2, half_len, R, LANES), BF16),
            pltpu.VMEM((chunks, half_len, R, LANES), BF16),
            pltpu.VMEM((chunks, R * count, 2 * LANES), F32),
            pltpu.VMEM((chunks, R * count, 2 * LANES), F32),
            pltpu.VMEM((chunks, 2 * LANES, total), BF16),
            pltpu.VMEM((rows, total), F32),
            pltpu.VMEM((T, 8, width), F32),
            pltpu.VMEM((8, width), F32),
            pltpu.VMEM((3, 2, 8, width), F32),
            pltpu.VMEM((chunks, 8, 2 * LANES), F32),
            pltpu.VMEM((2, R * count, 1), F32),
            pltpu.VMEM((8, 1), F32),
            dma((2, chunks)), dma((chunks,)), dma((chunks,)), dma((2, chunks)),
            dma((chunks,)), dma((chunks,)),
            dma((T,)), dma((T,)), dma((3, 2)), dma((3, 2)),
        ],
        compiler_params=pltpu.CompilerParams(
            collective_id=0, has_side_effects=True, vmem_limit_bytes=48 * 1024 * 1024),
        cost_estimate=pl.CostEstimate(
            flops=2 * rows * total * (total + 2 * R * count),
            bytes_accessed=8 * rows * total, transcendentals=0),
    )(pieces, wide, wide_t, ones, shifts, bands, memory)
    return out.reshape(half_len, R, total)


def solution(mesh):
    placed = (
        P(("groups", "tm"), "cuts", "col"),
        P(("groups", "tm")),
        P(("groups", "cuts")),
        P(("groups", "cuts")),
    )
    return jax.shard_map(
        local,
        mesh=mesh,
        in_specs=placed,
        out_specs=P(("groups", "tm", "col"), "cuts", None),
        check_vma=False,
    )
```

```python
import functools
import math

import jax
import jax.numpy as jnp
import ml_dtypes
import numpy as np
from jax import lax
from jax.experimental import pallas as pl
from jax.experimental.pallas import tpu as pltpu
from jax.sharding import PartitionSpec as P

BAND_FREQS = 64
MESH = pl.DeviceIdType.MESH
LANES = 128
DEPTH = 3
F32 = jnp.float32
BF16 = jnp.bfloat16


def tables(half_len, row_count):
    angle_count = 2 * half_len
    freq = np.arange(1, BAND_FREQS + 1, dtype=np.int64)[:, None]
    phase = (freq * np.arange(half_len, dtype=np.int64)[None, :]) % angle_count
    radians = phase.astype(np.float64) * (2.0 * math.pi / angle_count)
    waves = np.concatenate([np.cos(radians), np.sin(radians)], axis=0)
    count = 2 * BAND_FREQS
    wide = np.zeros((row_count, count, half_len, row_count), np.float64)
    ones = np.zeros((16, half_len, row_count), np.float64)
    for s in range(row_count):
        wide[s, :, :, s] = waves
        ones[s, :, s] = 1.0
    wide = wide.reshape(row_count * count, half_len * row_count)
    ones = ones.reshape(16, half_len * row_count)
    cast = lambda v: jnp.asarray(v.astype(np.float32).astype(ml_dtypes.bfloat16))
    return cast(wide), cast(wide.T), cast(ones)


def kernel(sizes, x_ref, wave_hbm, wave_t_hbm, ones_hbm, shift_ref, band_ref, memory_ref, out_ref,
           wave_ref, wave_t_ref, ones_ref, t_sem,
           held, own, part, other, ramp, acc, sums, est, near, cyc, gain_ref, weight,
           l_sem, z_send, c_send, recv, p_send, p_recv, s_send, s_recv, e_send, e_recv):
    T, C, R = sizes
    half_len, chunks, _, _ = x_ref.shape
    rows, width = half_len * R, chunks * LANES
    total = 2 * width
    tm = lax.axis_index("tm")
    cut = lax.axis_index("cuts")
    col = lax.axis_index("col")
    mate = 1 - col

    def mine(j):
        return pltpu.make_async_copy(x_ref.at[:, j], own.at[j], l_sem.at[0, j])

    def kept(j):
        return pltpu.make_async_copy(x_ref.at[:, j], held.at[j, 1], l_sem.at[1, j])

    def flat(ref):
        return ref.reshape(rows, LANES)

    for j in range(chunks):
        mine(j).start()
    load_ones = pltpu.make_async_copy(ones_hbm, ones_ref, t_sem.at[0])
    load_wave = pltpu.make_async_copy(wave_hbm, wave_ref, t_sem.at[1])
    load_wave_t = pltpu.make_async_copy(wave_t_hbm, wave_t_ref, t_sem.at[2])
    load_ones.start()
    load_wave.start()
    load_wave_t.start()

    barrier = pltpu.get_barrier_semaphore()

    def greet(**where):
        pl.semaphore_signal(barrier, inc=1, device_id=where, device_id_type=MESH)

    for step in range(1, T):
        greet(tm=lax.rem(tm + step, T))
    greet(col=mate)
    for delta in (-1, 1):
        @pl.when((cut + delta >= 0) & (cut + delta < C))
        def _():
            for c in range(2):
                greet(cuts=cut + delta, col=jnp.int32(c))
    cross_up = (col == 1) & (tm < T - 1)
    cross_down = (col == 0) & (tm > 0)

    @pl.when(cross_up)
    def _():
        greet(tm=tm + 1, col=jnp.int32(0))

    @pl.when(cross_down)
    def _():
        greet(tm=tm - 1, col=jnp.int32(1))

    one = lambda flag: jnp.where(flag, 1, 0).astype(jnp.int32)
    pl.semaphore_wait(
        barrier, T + 2 * one(cut > 0) + 2 * one(cut < C - 1) + one(cross_up) + one(cross_down)
    )

    def sum_copy(source, target):
        return pltpu.make_async_remote_copy(
            src_ref=sums.at[source], dst_ref=sums.at[source],
            send_sem=s_send.at[target], recv_sem=s_recv.at[source],
            device_id={"tm": target}, device_id_type=MESH)

    def bulk(j, source_col, send_sem, where):
        return pltpu.make_async_remote_copy(
            src_ref=x_ref.at[:, j],
            dst_ref=held.at[j, source_col],
            send_sem=send_sem.at[j], recv_sem=recv.at[source_col, j],
            device_id=where, device_id_type=MESH)

    def ahead(j):
        return bulk(j, col, z_send, {"tm": lax.rem(tm + 1, T), "col": jnp.int32(0)})

    def across(j):
        return bulk(j, jnp.int32(0), c_send, {"col": mate})

    @pl.when(tm < T - 1)
    def _():
        for j in range(min(DEPTH, chunks)):
            ahead(jnp.int32(j)).start()

    @pl.when(col == 0)
    def _():
        @pl.loop(0, chunks)
        def _(j):
            across(j).start()

    @pl.when(col == 1)
    def _():
        for j in range(chunks):
            kept(j).start()

    load_ones.wait()
    for j in range(chunks):
        mine(j).wait()
        sums[tm, :, j * LANES:(j + 1) * LANES] = jnp.dot(
            ones_ref[...], flat(own.at[j])[...], preferred_element_type=F32)[:8]

    for u in range(T):
        @pl.when(u > tm)
        def _():
            sum_copy(tm, jnp.int32(u)).start()

    @pl.when((col == 0) & (tm == 0))
    def _():
        held[...] = jnp.zeros_like(held)

    acc[...] = jnp.zeros_like(acc)

    count = 2 * BAND_FREQS
    index = lax.broadcasted_iota(jnp.int32, (R * count, 1), 0)
    band = jnp.zeros((R * count, 1), F32)
    for s in range(R):
        band = jnp.where(index // count == s, band_ref[s].astype(F32), band)
    freq = index % BAND_FREQS + 1
    wave = freq.astype(F32)
    gain = jnp.exp(-(wave * wave) / (2.0 * band * band)) * (2.0 / (2 * (rows // R)))
    gain_ref[0] = gain
    gain_ref[1] = jnp.where(freq % 2 == 1, -gain, gain)

    STEP = 32

    target = lax.broadcasted_iota(jnp.int32, (1, total), 1) - shift_ref[0]
    target = jnp.where(target < 0, target + total, target)
    target = jnp.where(target >= total, target - total, target)

    @pl.loop(0, chunks)
    def _(j):
        for c in range(2):
            @pl.loop(0, LANES // STEP)
            def _(k):
                m = lax.broadcasted_iota(jnp.int32, (STEP, total), 0) + (
                    c * width + j * LANES + k * STEP)
                lag = target - m
                lag = jnp.where(lag < 0, lag + total, lag)
                dist = jnp.minimum(lag, total - lag)
                wide = jnp.maximum(dist, 1).astype(F32)
                tap = jnp.where(
                    dist == 0, 0.25,
                    jnp.where((dist & 1) == 1, -1.0 / (math.pi**2 * wide * wide), 0.0))
                ramp[j, pl.ds(pl.multiple_of(c * LANES + k * STEP, STEP), STEP), :] = tap.astype(BF16)

    def part_copy(j):
        return pltpu.make_async_remote_copy(
            src_ref=part.at[j], dst_ref=other.at[j],
            send_sem=p_send.at[j], recv_sem=p_recv.at[j],
            device_id={"col": mate}, device_id_type=MESH)

    def gather(j):
        @pl.when((col == 1) | (tm > 0))
        def _():
            bulk(j, jnp.int32(0), z_send, {"col": mate}).wait_recv()

        @pl.when((col == 0) & (tm > 0))
        def _():
            bulk(j, jnp.int32(1), z_send, {"col": mate}).wait_recv()

        @pl.when(tm < T - 1)
        def _():
            ahead(j).wait_send()

            @pl.when(j + DEPTH < chunks)
            def _():
                ahead(j + DEPTH).start()

        @pl.when(col == 1)
        def _():
            kept(j).wait()

        both = jnp.concatenate([flat(held.at[j, c])[...] for c in range(2)], axis=1)
        part[j] = jnp.dot(wave_ref[...], both, preferred_element_type=F32)
        part_copy(j).start()

    load_wave.wait()
    load_wave_t.wait()
    gather(jnp.int32(0))

    line_index = lax.broadcasted_iota(jnp.int32, (8, 1), 0)
    decay = jnp.zeros((8, 1), F32)
    for s in range(R):
        decay = jnp.where(line_index == s, memory_ref[s], decay)
    est[...] = jnp.zeros_like(est)
    weight[...] = jnp.zeros_like(weight)
    for u in range(T):
        @pl.when(u < tm)
        def _():
            sum_copy(jnp.int32(u), lax.rem(tm + 1, T)).wait_recv()

        @pl.when(u <= tm)
        def _():
            both = sums[u] if u == 0 else sums[u - 1] + sums[u]
            est[...] = decay * est[...] + both * (1.0 / (2 * (rows // R)))
            weight[...] = decay * weight[...] + 1.0
    est[...] = est[...] / weight[...]
    near[1, col] = est[...]

    def est_copy(delta, to_col, from_col):
        return pltpu.make_async_remote_copy(
            src_ref=est, dst_ref=near.at[1 - delta, from_col],
            send_sem=e_send.at[1 - delta, to_col], recv_sem=e_recv.at[1 - delta, from_col],
            device_id={"cuts": cut + delta, "col": to_col}, device_id_type=MESH)

    est_copy(0, mate, col).start()
    for delta in (-1, 1):
        @pl.when((cut + delta >= 0) & (cut + delta < C))
        def _():
            for c in range(2):
                est_copy(delta, jnp.int32(c), col).start()

    est_copy(0, mate, mate).wait_recv()
    for delta in (-1, 1):
        @pl.when((cut - delta >= 0) & (cut - delta < C))
        def _():
            for c in range(2):
                pltpu.make_async_remote_copy(
                    src_ref=est, dst_ref=near.at[1 - delta, c],
                    send_sem=e_send.at[1 - delta, c], recv_sem=e_recv.at[1 - delta, c],
                    device_id={"cuts": cut - delta, "col": jnp.int32(c)},
                    device_id_type=MESH).wait_recv()

        @pl.when((cut - delta < 0) | (cut - delta >= C))
        def _():
            near[1 - delta] = jnp.zeros_like(near[1 - delta])

    for c in range(2):
        edge = [near[0, c, R - 1:R, :]] + [near[1, c, s:s + 1, :] for s in range(R)] + [near[2, c, 0:1, :]]
        for s in range(R):
            line = (edge[s] + 2.0 * edge[s + 1] + edge[s + 2]) * 0.25
            for j in range(chunks):
                cyc[j, s:s + 1, c * LANES:(c + 1) * LANES] = line[:, j * LANES:(j + 1) * LANES]

    TILE = 256

    def filt(j, last):
        part_copy(j).wait_recv()
        scaled = (gain_ref[0] * part[j] + gain_ref[1] * other[j]).astype(BF16)
        which = lax.broadcasted_iota(jnp.int32, (TILE, 2 * LANES), 0) % R
        shade = jnp.zeros((TILE, 2 * LANES), F32)
        for s in range(R):
            shade = jnp.where(which == s, cyc[j, s:s + 1, :], shade)

        @pl.loop(0, rows // TILE)
        def _(k):
            tile = pl.ds(pl.multiple_of(k * TILE, TILE), TILE)
            low = jnp.dot(wave_t_ref[tile, :], scaled, preferred_element_type=F32)
            both = jnp.concatenate([flat(held.at[j, c])[tile, :] for c in range(2)], axis=1)
            damped = (both.astype(F32) - low - shade).astype(BF16)
            product = acc[tile, :] + jnp.dot(damped, ramp[j], preferred_element_type=F32)
            if last:
                out_ref[tile, :] = product.astype(BF16)
            else:
                acc[tile, :] = product

    @pl.loop(1, chunks)
    def _(j):
        gather(j)
        filt(j - 1, False)

    filt(chunks - 1, True)

    for u in range(T):
        @pl.when(u > tm)
        def _():
            sum_copy(tm, jnp.int32(u)).wait_send()
    est_copy(0, mate, col).wait_send()
    for delta in (-1, 1):
        @pl.when((cut + delta >= 0) & (cut + delta < C))
        def _():
            for c in range(2):
                est_copy(delta, jnp.int32(c), col).wait_send()

    @pl.loop(0, chunks)
    def _(j):
        part_copy(j).wait_send()

        @pl.when(col == 0)
        def _():
            across(j).wait_send()


def local(turns, shifts, bands, memory):
    half_len, R, width = turns.shape
    T, C = lax.axis_size("tm"), lax.axis_size("cuts")
    rows, total, chunks = half_len * R, 2 * width, width // LANES
    count = 2 * BAND_FREQS
    wide, wide_t, ones = tables(half_len, R)
    pieces = turns.reshape(half_len, R, chunks, LANES).transpose(0, 2, 1, 3)

    vmem = pl.BlockSpec(memory_space=pltpu.VMEM)
    dma = pltpu.SemaphoreType.DMA
    out = pl.pallas_call(
        functools.partial(kernel, (T, C, R)),
        out_shape=jax.ShapeDtypeStruct((rows, total), BF16),
        in_specs=[pl.BlockSpec(memory_space=pltpu.HBM)] * 4 + [pl.BlockSpec(memory_space=pltpu.SMEM)] * 3,
        out_specs=vmem,
        scratch_shapes=[
            pltpu.VMEM(wide.shape, BF16), pltpu.VMEM(wide_t.shape, BF16), pltpu.VMEM(ones.shape, BF16), dma((3,)),
            pltpu.VMEM((chunks, 2, half_len, R, LANES), BF16),
            pltpu.VMEM((chunks, half_len, R, LANES), BF16),
            pltpu.VMEM((chunks, R * count, 2 * LANES), F32),
            pltpu.VMEM((chunks, R * count, 2 * LANES), F32),
            pltpu.VMEM((chunks, 2 * LANES, total), BF16),
            pltpu.VMEM((rows, total), F32),
            pltpu.VMEM((T, 8, width), F32),
            pltpu.VMEM((8, width), F32),
            pltpu.VMEM((3, 2, 8, width), F32),
            pltpu.VMEM((chunks, 8, 2 * LANES), F32),
            pltpu.VMEM((2, R * count, 1), F32),
            pltpu.VMEM((8, 1), F32),
            dma((2, chunks)), dma((chunks,)), dma((chunks,)), dma((2, chunks)),
            dma((chunks,)), dma((chunks,)),
            dma((T,)), dma((T,)), dma((3, 2)), dma((3, 2)),
        ],
        compiler_params=pltpu.CompilerParams(
            collective_id=0, has_side_effects=True, vmem_limit_bytes=60 * 1024 * 1024),
        cost_estimate=pl.CostEstimate(
            flops=2 * rows * total * (total + 2 * R * count),
            bytes_accessed=8 * rows * total, transcendentals=0),
    )(pieces, wide, wide_t, ones, shifts, bands, memory)
    return out.reshape(half_len, R, total)


def solution(mesh):
    placed = (
        P(("groups", "tm"), "cuts", "col"),
        P(("groups", "tm")),
        P(("groups", "cuts")),
        P(("groups", "cuts")),
    )
    return jax.shard_map(
        local,
        mesh=mesh,
        in_specs=placed,
        out_specs=P(("groups", "tm", "col"), "cuts", None),
        check_vma=False,
    )
```
